32 devices in a mesh: prow: 4 (over y, x), pcol: 8 (over z, core).
Axes of the slice: x: 2, y: 2, z: 4, core: 2. Of those that a mesh axis runs over, the one named last changes fastest.
Arguments:
- panel: bfloat16 [4, 4, 512, 512], P(None, 'prow', 'pcol'), may hold values from -1.5 to 1.5
- diag_inv: bfloat16 [512, 512], replicated, as said below
- nonzero: int32 [4, 4], P(None, 'prow'), may hold values from 0 to 1
- trailing: bfloat16 [4, 4, 1, 8, 512, 512], P(None, 'prow', None, 'pcol'), may hold values from -6 to 6
Outputs:
- panel_factor: bfloat16 [4, 4, 512, 512], P(None, 'prow', 'pcol')
- trailing_out: bfloat16 [4, 4, 1, 8, 512, 512], P(None, 'prow', None, 'pcol')
The draws below stay inside these ranges and needn't reach their ends.
Inputs may be any that keep to these rules, and one draw needn't show every extreme that they name: `diag_inv`: lower triangular with a positive diagonal.
All inputs are finite; a program needn't handle non-finite values.
Results may differ from the reference program's by a relative error of at most 0.0017.
Values may be sent and summed in bfloat16 or wider, within the bound.
No kernel may reach another device: no remote copies, remote signals or barrier semaphores. Data moves between devices by JAX's collectives and lax.ppermute only.
A program may use at most 64 MiB of HBM per device.

```python
import math
import jax
import jax.numpy as jnp
from jax import lax

B = 512
ROWS_DEV = 4
COLS_DEV = 1
GRID_ROWS = 4
GRID_COLS = 8
NR = 16
NC = 8


def draw_diag_inv(key, part):
    first_key, second_key = jax.random.split(jax.random.fold_in(key, 11))
    row_ids = lax.broadcasted_iota(jnp.int32, (B, B), 0)
    col_ids = lax.broadcasted_iota(jnp.int32, (B, B), 1)
    diagonal = jnp.exp(jax.random.uniform(first_key, (B,), jnp.float32, -1.0, 0.0))
    below = jax.random.normal(second_key, (B, B), jnp.float32) * 0.7 / math.sqrt(B)
    lower_part = jnp.where(row_ids > col_ids, below, 0.0)
    diag_part = jnp.where(row_ids == col_ids, diagonal[:, None], 0.0)
    return (lower_part + diag_part).astype(jnp.bfloat16)


def draw_nonzero(key, part):
    shape_pair = (ROWS_DEV, NR // ROWS_DEV)
    tile_ids = lax.broadcasted_iota(jnp.int32, shape_pair, 0) * (NR // ROWS_DEV) + lax.broadcasted_iota(jnp.int32, shape_pair, 1)
    picked = jax.random.randint(jax.random.fold_in(key, 23), shape_pair, 0, NR)
    return jnp.where(picked >= tile_ids, 1, 0).astype(jnp.int32)


def levels(key, extent, cuts, least, top_value):
    def one(dim, parts):
        draws = jax.random.uniform(jax.random.fold_in(jax.random.fold_in(key, 6), dim), (parts,), jnp.float32, least / len(cuts), top_value / len(cuts))
        return jnp.repeat(jnp.exp(draws), extent[dim] // parts).reshape((-1,) + (1,) * (len(extent) - dim - 1))

    factor_of = one(*cuts[0])
    for cut in cuts[1:]:
        factor_of = factor_of * one(*cut)
    return factor_of


def normal_values(own_key, dims, width, reach, shards=(), held_as=jnp.bfloat16):
    values = jax.random.normal(own_key, dims, jnp.float32) * width
    if len(shards) > 0:
        values = levels(own_key, dims, shards, -0.22, 0.18) * values
    return jnp.clip(values, min=-reach, max=reach).astype(held_as)


def setup_inputs(seed: int = 0) -> dict:
    keys = jax.random.split(jax.random.key(seed), 5)
    return {
        "panel": normal_values(keys[0], (ROWS_DEV, GRID_ROWS, B, B), 0.25, 1.5, ((1, 4), (2, 8))),
        "diag_inv": draw_diag_inv(jax.random.fold_in(keys[4], 71), 0),
        "nonzero": draw_nonzero(jax.random.fold_in(keys[4], 71), 0),
        "trailing": normal_values(keys[3], (ROWS_DEV, GRID_ROWS, COLS_DEV, GRID_COLS, B, B), 1.0, 6.0, ((1, 4), (3, 8))),
    }


def reference(panel, diag_inv, nonzero, trailing):
    tile_size = diag_inv.shape[0]
    blocks = panel.reshape(NR, tile_size, tile_size).astype(jnp.float32)
    live_rows = nonzero.reshape(NR).astype(jnp.float32)
    inverse = diag_inv.astype(jnp.float32)
    solved = jnp.einsum("inb,ab->ina", blocks, inverse, precision=lax.Precision.HIGHEST)
    factor = (solved * live_rows[:, None, None]).astype(jnp.bfloat16)
    column_tiles = factor[:NC].reshape(COLS_DEV, GRID_COLS, tile_size, tile_size).astype(jnp.float32)
    column_ids = (lax.broadcasted_iota(jnp.int32, (COLS_DEV, GRID_COLS), 0) * GRID_COLS
                  + lax.broadcasted_iota(jnp.int32, (COLS_DEV, GRID_COLS), 1))
    stacked = trailing.reshape(NR, COLS_DEV, GRID_COLS, tile_size, tile_size)

    def one_row(operands):
        row_id, row_tile, previous = operands
        product = jnp.einsum("na,tcba->tcnb", row_tile.astype(jnp.float32), column_tiles,
                             precision=lax.Precision.HIGHEST)
        updated = (previous.astype(jnp.float32) - product).astype(jnp.bfloat16)
        return jnp.where((row_id >= column_ids)[:, :, None, None], updated, previous)

    renewed = lax.map(one_row, (jnp.arange(NR, dtype=jnp.int32), factor, stacked))
    return factor.reshape(ROWS_DEV, GRID_ROWS, tile_size, tile_size), renewed.reshape(trailing.shape)
```

```python
import functools

import jax
import jax.numpy as jnp
from jax import lax
from jax.experimental import pallas as pl
from jax.experimental.pallas import tpu as pltpu
from jax.sharding import PartitionSpec as P

TRANSPOSED = (((1,), (1,)), ((), ()))
HBM = pl.BlockSpec(memory_space=pl.ANY)
VMEM = pl.BlockSpec(memory_space=pltpu.VMEM)
SMEM = pl.BlockSpec(memory_space=pltpu.SMEM)
LIMIT = 60 * 1024 * 1024
SMALL = 8 * 1024 * 1024


def swap(x, axis, distance):
    size = lax.axis_size(axis)
    return lax.ppermute(x, axis, [(i, i ^ distance) for i in range(size)])


def solve_kernel(classes, nonzero, panel, diag_inv, factor, *refs):
    slabs, rests = refs[:classes], refs[classes:2 * classes]
    live, strips, inverse, sems = refs[2 * classes:]
    copies = [pltpu.make_async_copy(*pair, sems.at[n])
              for n, pair in enumerate(((nonzero, live), (panel, strips), (diag_inv, inverse)))]
    for copy in copies:
        copy.start()
    for copy in copies:
        copy.wait()
    steps, _, rows, size = strips.shape
    tiles_in = strips[...].reshape(steps * rows, size)
    product = lax.dot_general(tiles_in, inverse[...], TRANSPOSED, preferred_element_type=jnp.float32)
    product = product.reshape(steps, rows, size)
    for s in range(steps):
        factor[s, 0] = (product[s] * live[s].astype(jnp.float32)).astype(factor.dtype)
    own = lax.axis_index("pcol") // lax.axis_size("prow")
    for n in range(classes):
        first = jnp.bitwise_xor(own, n)
        slabs[n][...] = factor[first, 0]
        for m in range(1, steps):
            rests[n][m - 1] = factor[lax.rem(first + m, steps), 0]


def solve(panel, diag_inv, nonzero, classes):
    steps, _, rows, size = panel.shape
    slab = jax.ShapeDtypeStruct((rows, size), panel.dtype)
    rest = jax.ShapeDtypeStruct((steps - 1, rows, size), panel.dtype)
    outs = pl.pallas_call(
        functools.partial(solve_kernel, classes),
        out_shape=[jax.ShapeDtypeStruct(panel.shape, panel.dtype)] + [slab] * classes + [rest] * classes,
        in_specs=[HBM, HBM, HBM],
        out_specs=[VMEM] * (1 + 2 * classes),
        scratch_shapes=[
            pltpu.SMEM(nonzero[:, 0].shape, nonzero.dtype),
            pltpu.VMEM(panel.shape, panel.dtype),
            pltpu.VMEM(diag_inv.shape, diag_inv.dtype),
            pltpu.SemaphoreType.DMA((3,)),
        ],
        cost_estimate=pl.CostEstimate(flops=0, bytes_accessed=1024, transcendentals=0),
        compiler_params=pltpu.CompilerParams(vmem_limit_bytes=LIMIT),
        name="solve",
    )(nonzero[:, 0], panel, diag_inv)
    return outs[0], outs[1:1 + classes], outs[1 + classes:]


def pick_kernel(sources, *refs):
    ins, (keep, give) = refs[:sources], refs[sources:]
    c, r = lax.axis_index("pcol"), lax.axis_index("prow")
    for target, column in ((keep, c), (give, jnp.bitwise_xor(c, 1))):
        away = jnp.bitwise_xor(r, lax.rem(column, sources))
        for k in range(sources):
            @pl.when(away == k)
            def _():
                target[...] = ins[k][...]


def pick(slabs):
    shape = jax.ShapeDtypeStruct(slabs[0].shape, slabs[0].dtype)
    return pl.pallas_call(
        functools.partial(pick_kernel, len(slabs)),
        out_shape=[shape, shape],
        in_specs=[VMEM] * len(slabs),
        out_specs=[VMEM, VMEM],
        cost_estimate=pl.CostEstimate(flops=0, bytes_accessed=1024, transcendentals=0),
        compiler_params=pltpu.CompilerParams(vmem_limit_bytes=SMALL),
        name="pick",
    )(*slabs)


def renew_kernel(chips, *refs):
    firsts, rests, columns = refs[:2], refs[2:2 + 2 * chips], refs[2 + 2 * chips:4 + 2 * chips]
    trailing, out, rows_full, column, held, strip_sems, column_sems, in_sems, out_sems = refs[4 + 2 * chips:]
    steps, size = held.shape[0], held.shape[1]
    rows = firsts[0].shape[1]
    c, r = lax.axis_index("pcol"), lax.axis_index("prow")
    grid_rows = lax.axis_size("prow")
    own = c // grid_rows
    order = [lax.rem(own + m, steps) for m in range(steps)]

    def offset(core, k):
        source = jnp.bitwise_xor(c, 2 * k + core)
        return pl.ds(pl.multiple_of(source * rows, rows), rows)

    column_copies, strip_copies, in_copies = [], [], []
    for core in range(2):
        for k in range(chips):
            n = core * chips + k
            column_copies.append(pltpu.make_async_copy(columns[core].at[k], column.at[offset(core, k)], column_sems.at[n]))
    for copy in column_copies:
        copy.start()
    for m in range(steps):
        these = []
        for core in range(2):
            for k in range(chips):
                n = core * chips + k
                source = firsts[core].at[k] if m == 0 else rests[n].at[m - 1]
                these.append(pltpu.make_async_copy(source, rows_full.at[m, offset(core, k)], strip_sems.at[m, n]))
        strip_copies.append(these)
        in_copies.append(pltpu.make_async_copy(trailing.at[order[m], 0, 0, 0], held.at[m], in_sems.at[m]))
        for copy in these + in_copies[-1:]:
            copy.start()
    for copy in column_copies:
        copy.wait()
    for m in range(steps):
        for copy in strip_copies[m]:
            copy.wait()
        in_copies[m].wait()

        @pl.when(order[m] * grid_rows + r >= c)
        def _():
            product = lax.dot_general(rows_full[m], column[...], TRANSPOSED, preferred_element_type=jnp.float32)
            held[m] = (held[m].astype(jnp.float32) - product).astype(held.dtype)

        pltpu.make_async_copy(held.at[m], out.at[order[m], 0, 0, 0], out_sems.at[m]).start()
    for m in range(steps):
        pltpu.make_async_copy(held.at[m], out.at[order[m], 0, 0, 0], out_sems.at[m]).wait()


def renew(trailing, firsts, rests, columns):
    chips = len(rests) // 2
    steps, size = trailing.shape[0], trailing.shape[-1]
    tiles = pltpu.VMEM((steps, size, size), trailing.dtype)
    return pl.pallas_call(
        functools.partial(renew_kernel, chips),
        out_shape=jax.ShapeDtypeStruct(trailing.shape, trailing.dtype),
        in_specs=[HBM] * (5 + 2 * chips),
        out_specs=HBM,
        scratch_shapes=[
            tiles,
            pltpu.VMEM((size, size), trailing.dtype),
            tiles,
            pltpu.SemaphoreType.DMA((steps, 2 * chips)),
            pltpu.SemaphoreType.DMA((2 * chips,)),
            pltpu.SemaphoreType.DMA((steps,)),
            pltpu.SemaphoreType.DMA((steps,)),
        ],
        compiler_params=pltpu.CompilerParams(vmem_limit_bytes=LIMIT),
        name="renew",
    )(*firsts, *rests, *columns, trailing)


def body(panel, diag_inv, nonzero, trailing):
    grid_rows, grid_cols = lax.axis_size("prow"), lax.axis_size("pcol")
    chips = grid_cols // 2
    classes = max(1, grid_cols // grid_rows)
    factor, slabs, rests = solve(panel, diag_inv, nonzero, classes)

    def kind(k):
        return 2 * k // grid_rows

    near = [slabs[0]] + [swap(slabs[kind(k)], "pcol", 2 * k) for k in range(1, chips)]
    first = jnp.stack(near)
    rest = {0: rests[0]}
    for k in range(1, chips):
        low = k & -k
        if low == k:
            rest[k] = swap(rests[kind(k)], "pcol", 2 * k)
        else:
            rest[k] = None
    for k in range(1, chips):
        if rest[k] is None:
            low = k & -k
            rest[k] = swap(rests[kind(k)], "pcol", 2 * k) if RELAY == 0 else swap(rest[k ^ low], "pcol", 2 * low)
    spread = [first] + [swap(first, "prow", k) for k in range(1, grid_rows)]
    keep, give = pick(spread)
    columns = [keep, swap(give, "pcol", 1)]
    firsts = [first, swap(first, "pcol", 1)]
    own_rest = [rest[k] for k in range(chips)]
    other_rest = [swap(x, "pcol", 1) for x in own_rest]
    renewed = renew(trailing, firsts, own_rest + other_rest, columns)
    return factor, renewed


RELAY = 1


def solution(mesh):
    placed = (
        P(None, "prow", "pcol", None),
        P(),
        P(None, "prow"),
        P(None, "prow", None, "pcol", None, None),
    )
    return jax.shard_map(
        body,
        mesh=mesh,
        in_specs=placed,
        out_specs=(P(None, "prow", "pcol", None), P(None, "prow", None, "pcol", None, None)),
        check_vma=False,
    )
```

```python
import functools

import jax
import jax.numpy as jnp
from jax import lax
from jax.experimental import pallas as pl
from jax.experimental.pallas import tpu as pltpu
from jax.sharding import PartitionSpec as P

TRANSPOSED = (((1,), (1,)), ((), ()))
HBM = pl.BlockSpec(memory_space=pl.ANY)
VMEM = pl.BlockSpec(memory_space=pltpu.VMEM)
SMEM = pl.BlockSpec(memory_space=pltpu.SMEM)
LIMIT = 16 * 1024 * 1024
SOLVE = 62914560
SMALL = 8 * 1024 * 1024


def swap(x, axis, distance):
    size = lax.axis_size(axis)
    return lax.ppermute(x, axis, [(i, i ^ distance) for i in range(size)])


def solve_kernel(classes, nonzero, panel, diag_inv, factor, *refs):
    slabs, rests = refs[:classes], refs[classes:2 * classes]
    live, strips, inverse, sems = refs[2 * classes:]
    copies = [pltpu.make_async_copy(*pair, sems.at[n])
              for n, pair in enumerate(((nonzero, live), (panel, strips), (diag_inv, inverse)))]
    for copy in copies:
        copy.start()
    for copy in copies:
        copy.wait()
    steps, _, rows, size = strips.shape
    tiles_in = strips[...].reshape(steps * rows, size)
    product = lax.dot_general(tiles_in, inverse[...], TRANSPOSED, preferred_element_type=jnp.float32)
    product = product.reshape(steps, rows, size)
    for s in range(steps):
        factor[s, 0] = (product[s] * live[s].astype(jnp.float32)).astype(factor.dtype)
    own = lax.axis_index("pcol") // lax.axis_size("prow")
    for n in range(classes):
        first = jnp.bitwise_xor(own, n)
        slabs[n][0] = factor[first, 0]
        for m in range(1, steps):
            rests[n][m - 1] = factor[lax.rem(first + m, steps), 0]


def solve(panel, diag_inv, nonzero, classes):
    steps, _, rows, size = panel.shape
    slab = jax.ShapeDtypeStruct((1, rows, size), panel.dtype)
    rest = jax.ShapeDtypeStruct((steps - 1, rows, size), panel.dtype)
    outs = pl.pallas_call(
        functools.partial(solve_kernel, classes),
        out_shape=[jax.ShapeDtypeStruct(panel.shape, panel.dtype)] + [slab] * classes + [rest] * classes,
        in_specs=[pl.BlockSpec(memory_space=pltpu.HBM)] * 3,
        out_specs=[VMEM] * (1 + 2 * classes),
        scratch_shapes=[
            pltpu.SMEM(nonzero[:, 0].shape, nonzero.dtype),
            pltpu.VMEM(panel.shape, panel.dtype),
            pltpu.VMEM(diag_inv.shape, diag_inv.dtype),
            pltpu.SemaphoreType.DMA((3,)),
        ],
        cost_estimate=pl.CostEstimate(flops=0, bytes_accessed=1024, transcendentals=0),
        compiler_params=pltpu.CompilerParams(vmem_limit_bytes=SOLVE),
        name="solve",
    )(nonzero[:, 0], panel, diag_inv)
    return outs[0], outs[1:1 + classes], outs[1 + classes:]


def pick_kernel(sources, *refs):
    ins, (keep, packed) = refs[:sources], refs[sources:]
    span = ins[0].shape[0]
    c, r = lax.axis_index("pcol"), lax.axis_index("prow")
    packed[span:] = ins[0][...]
    for k in range(sources):
        @pl.when(jnp.bitwise_xor(r, lax.rem(c, sources)) == k)
        def _():
            keep[...] = ins[k][...]

        @pl.when(jnp.bitwise_xor(r, lax.rem(jnp.bitwise_xor(c, 1), sources)) == k)
        def _():
            packed[:span] = ins[k][...]


def pick(slabs):
    span, *rest = slabs[0].shape
    outs = [jax.ShapeDtypeStruct(slabs[0].shape, slabs[0].dtype), jax.ShapeDtypeStruct((2 * span, *rest), slabs[0].dtype)]
    return small_call(functools.partial(pick_kernel, len(slabs)), outs, slabs, "pick")


def small_call(kernel, outs, args, name):
    return pl.pallas_call(
        kernel,
        out_shape=outs,
        in_specs=[VMEM] * len(args),
        out_specs=jax.tree.map(lambda _: VMEM, outs),
        cost_estimate=pl.CostEstimate(flops=0, bytes_accessed=1024, transcendentals=0),
        compiler_params=pltpu.CompilerParams(vmem_limit_bytes=SMALL),
        name=name,
    )(*args)


def choose_kernel(bit, mine, came, out):
    away = jnp.bitwise_xor(lax.axis_index("prow"), lax.rem(lax.axis_index("pcol"), lax.axis_size("prow")))
    here = jnp.bitwise_and(away, bit) == 0

    @pl.when(here)
    def _():
        out[...] = mine[...]

    @pl.when(jnp.logical_not(here))
    def _():
        out[...] = came[...]


def choose(bit, mine, came):
    shape = jax.ShapeDtypeStruct(mine.shape, mine.dtype)
    return small_call(functools.partial(choose_kernel, bit), shape, (mine, came), "choose")


def pack_kernel(mine, came, first, keep, packed):
    span = first.shape[0]
    here = lax.rem(lax.axis_index("prow"), 2) == lax.rem(lax.axis_index("pcol"), 2)
    packed[span:] = first[...]

    @pl.when(here)
    def _():
        keep[...] = mine[...]
        packed[:span] = came[...]

    @pl.when(jnp.logical_not(here))
    def _():
        keep[...] = came[...]
        packed[:span] = mine[...]


def pack(mine, came, first):
    span, *rest = first.shape
    outs = [jax.ShapeDtypeStruct(first.shape, first.dtype), jax.ShapeDtypeStruct((2 * span, *rest), first.dtype)]
    return small_call(pack_kernel, outs, (mine, came, first), "pack")


def join_kernel(*refs):
    at = 0
    for ref in refs[:-1]:
        refs[-1][at:at + ref.shape[0]] = ref[...]
        at += ref.shape[0]


def join(parts):
    total = sum(x.shape[0] for x in parts)
    return small_call(join_kernel, jax.ShapeDtypeStruct((total, *parts[0].shape[1:]), parts[0].dtype), parts, "join")


def hold_kernel(x, _, out):
    del x, out


def hold(x, until):
    return pl.pallas_call(
        hold_kernel,
        out_shape=jax.ShapeDtypeStruct(x.shape, x.dtype),
        in_specs=[HBM, HBM],
        out_specs=HBM,
        input_output_aliases={0: 0},
        cost_estimate=pl.CostEstimate(flops=0, bytes_accessed=1024, transcendentals=0),
        compiler_params=pltpu.CompilerParams(vmem_limit_bytes=SMALL),
        name="hold",
    )(x, until)


def renew_kernel(chips, groups, *refs):
    firsts, keeps, gots = refs[:groups], refs[groups:2 * groups], refs[2 * groups:3 * groups]
    rests, others = refs[3 * groups:3 * groups + chips - 1], refs[3 * groups + chips - 1:-6]
    trailing, out, rows_full, column, held, out_sems = refs[-6:]
    steps = held.shape[0]
    span, rows = firsts[0].shape[0], firsts[0].shape[1]
    c, r = lax.axis_index("pcol"), lax.axis_index("prow")
    grid_rows = lax.axis_size("prow")
    own = c // grid_rows
    order = [lax.rem(own + m, steps) for m in range(steps)]
    for core in range(2):
        for k in range(chips):
            source = jnp.bitwise_xor(c, 2 * k + core)
            here = pl.ds(pl.multiple_of(source * rows, rows), rows)
            n, at = k // span, k % span
            if core == 0:
                column[here] = keeps[n][at]
                rows_full[0, here] = firsts[n][at]
            else:
                column[here] = gots[n][at]
                rows_full[0, here] = gots[n][span + at]
            for m in range(1, steps):
                parts = (rests, others)[core]
                rows_full[m, here] = parts[0][k * (steps - 1) + m - 1] if k < 2 else parts[k - 1][m - 1]
    for m in range(steps):
        active = order[m] * grid_rows + r >= c

        @pl.when(active)
        def _():
            product = lax.dot_general(rows_full[m], column[...], TRANSPOSED, preferred_element_type=jnp.float32)
            before = trailing[order[m], 0, 0, 0].astype(jnp.float32)
            held[m] = (before - product).astype(held.dtype)

        @pl.when(jnp.logical_not(active))
        def _():
            held[m] = trailing[order[m], 0, 0, 0]

        pltpu.make_async_copy(held.at[m], out.at[order[m], 0, 0, 0], out_sems.at[m]).start()
    for m in range(steps):
        pltpu.make_async_copy(held.at[m], out.at[order[m], 0, 0, 0], out_sems.at[m]).wait()


def renew(trailing, firsts, keeps, gots, rests, others):
    chips, groups = len(rests) + 1, len(firsts)
    steps, size = trailing.shape[0], trailing.shape[-1]
    tiles = pltpu.VMEM((steps, size, size), trailing.dtype)
    args = (*firsts, *keeps, *gots, *rests, *others, trailing)
    return pl.pallas_call(
        functools.partial(renew_kernel, chips, groups),
        out_shape=jax.ShapeDtypeStruct(trailing.shape, trailing.dtype),
        in_specs=[VMEM] * len(args),
        out_specs=HBM,
        scratch_shapes=[
            tiles,
            pltpu.VMEM((size, size), trailing.dtype),
            tiles,
            pltpu.SemaphoreType.DMA((steps,)),
        ],
        compiler_params=pltpu.CompilerParams(vmem_limit_bytes=LIMIT),
        name="renew",
    )(*args)


def body(panel, diag_inv, nonzero, trailing):
    grid_rows, grid_cols = lax.axis_size("prow"), lax.axis_size("pcol")
    chips = grid_cols // 2
    classes = max(1, grid_cols // grid_rows)
    factor, slabs, rests = solve(panel, diag_inv, nonzero, classes)
    slabs, rests = list(slabs), list(rests)

    def kind(k):
        return 2 * k // grid_rows

    def gather(parts, relay, gates):
        held = [parts[0]]
        for k in range(1, chips):
            low = k & -k
            relayed = relay and low != k and kind(low) == 0
            if k in gates:
                if relayed:
                    held[k ^ low] = hold(held[k ^ low], gates[k](held))
                else:
                    parts[kind(k)] = hold(parts[kind(k)], gates[k](held))
                    held[0] = parts[0]
            source = held[k ^ low] if relayed else parts[kind(k)]
            held.append(swap(source, "pcol", 2 * low if relayed else 2 * k))
        return held

    top = chips // 2
    near = gather(slabs, PREL, {top + 1: lambda held: held[1]} if G3 else {})
    half = max(1, chips // GROUPS)
    firsts = [join(near[n:n + half]) for n in range(0, chips, half)]
    marks = {"p1": near[1], "p2": near[top], "p3": near[-1], "b": firsts[-1], "a": firsts[0]}
    gates = {}
    if G2:
        gates[top] = lambda held: marks[G2]
    if G1:
        gates[1] = lambda held: marks[G1]
    rest = gather(rests, QREL, gates)
    keeps, gots = [], []
    for first in firsts:
        if XY == "hyper":
            mine = first
            bit = grid_rows // 2
            while bit > 1:
                mine = choose(bit, mine, swap(mine, "prow", bit))
                bit //= 2
            keep, packed = pack(mine, swap(mine, "prow", 1), first)
        else:
            keep, packed = pick([first] + [swap(first, "prow", k) for k in range(1, grid_rows)])
        keeps.append(keep)
        gots.append(swap(packed, "pcol", 1))
    pair = join(rest[:2])
    others = [swap(pair, "pcol", 1)] + [swap(x, "pcol", 1) for x in rest[2:]]
    renewed = renew(trailing, firsts, keeps, gots, [pair] + rest[2:], others)
    return factor, renewed


PREL = True
QREL = True
GROUPS = 2
G1 = None
G2 = None
G3 = False
XY = 'hyper'


def solution(mesh):
    placed = (
        P(None, "prow", "pcol", None),
        P(),
        P(None, "prow"),
        P(None, "prow", None, "pcol", None, None),
    )
    return jax.shard_map(
        body,
        mesh=mesh,
        in_specs=placed,
        out_specs=(P(None, "prow", "pcol", None), P(None, "prow", None, "pcol", None, None)),
        check_vma=False,
    )
```

```python
import functools

import jax
import jax.numpy as jnp
from jax import lax
from jax.experimental import pallas as pl
from jax.experimental.pallas import tpu as pltpu
from jax.sharding import PartitionSpec as P

TRANSPOSED = (((1,), (1,)), ((), ()))
HBM = pl.BlockSpec(memory_space=pl.ANY)
VMEM = pl.BlockSpec(memory_space=pltpu.VMEM)
SMEM = pl.BlockSpec(memory_space=pltpu.SMEM)
LIMIT = 16 * 1024 * 1024
FIRST = 56418304
SOLVE = 62914560
SMALL = 8 * 1024 * 1024


def swap(x, axis, distance):
    size = lax.axis_size(axis)
    return lax.ppermute(x, axis, [(i, i ^ distance) for i in range(size)])


def load(pairs, sems):
    copies = [pltpu.make_async_copy(*pair, sems.at[n]) for n, pair in enumerate(pairs)]
    for copy in copies:
        copy.start()
    for copy in copies:
        copy.wait()


def first_kernel(classes, panel, diag_inv, *refs):
    slabs, (strips, inverse, sems) = refs[:classes], refs[classes:]
    own = lax.axis_index("pcol") // lax.axis_size("prow")
    load([(diag_inv, inverse)]
         + [(panel.at[jnp.bitwise_xor(own, n), 0], strips.at[n]) for n in range(classes)], sems)
    rows, size = strips.shape[1:]
    product = lax.dot_general(strips[...].reshape(classes * rows, size), inverse[...], TRANSPOSED,
                              preferred_element_type=jnp.float32).reshape(classes, rows, size)
    for n in range(classes):
        slabs[n][0] = product[n].astype(strips.dtype)


def rest_kernel(classes, nonzero, panel, diag_inv, factor, mask, *refs):
    rests, (live, strips, inverse, sems) = refs[:-4], refs[-4:]
    load([(nonzero, live), (panel, strips), (diag_inv, inverse)], sems)
    steps, _, rows, size = strips.shape
    product = lax.dot_general(strips[...].reshape(steps * rows, size), inverse[...], TRANSPOSED,
                              preferred_element_type=jnp.float32).reshape(steps, rows, size)
    for s in range(steps):
        factor[s, 0] = (product[s] * live[s].astype(jnp.float32)).astype(factor.dtype)
    own = lax.axis_index("pcol") // lax.axis_size("prow")
    mask[...] = jnp.full(mask.shape, live[own].astype(jnp.float32), mask.dtype)
    at = 0
    for n in range(classes):
        m = 1
        while m < steps:
            for i in range(rests[at].shape[0]):
                rests[at][i] = factor[lax.rem(jnp.bitwise_xor(own, n) + m + i, steps), 0]
            m += rests[at].shape[0]
            at += 1


def solve_call(kernel, outs, scratch, copies, limit, args, name):
    return pl.pallas_call(
        kernel,
        out_shape=outs,
        in_specs=[pl.BlockSpec(memory_space=pltpu.HBM)] * len(args),
        out_specs=[VMEM] * len(outs),
        scratch_shapes=scratch + [pltpu.SemaphoreType.DMA((copies,))],
        cost_estimate=pl.CostEstimate(flops=0, bytes_accessed=1024, transcendentals=0),
        compiler_params=pltpu.CompilerParams(vmem_limit_bytes=limit),
        name=name,
    )(*args)


def solve(panel, diag_inv, nonzero, classes):
    steps, _, rows, size = panel.shape
    dtype = panel.dtype
    slab = jax.ShapeDtypeStruct((1, rows, size), dtype)
    cuts = [[steps - 1]] + [CUTS(steps)] * (classes - 1)
    rest = [jax.ShapeDtypeStruct((n, rows, size), dtype) for cut in cuts for n in cut]
    mask = jax.ShapeDtypeStruct((1, size), jnp.float32)
    inverse = pltpu.VMEM(diag_inv.shape, dtype)
    slabs = solve_call(functools.partial(first_kernel, classes), [slab] * classes,
                       [pltpu.VMEM((classes, rows, size), dtype), inverse], 1 + classes, FIRST,
                       (panel, diag_inv), "solve_first")
    factor, mask, *rests = solve_call(functools.partial(rest_kernel, classes),
                                      [jax.ShapeDtypeStruct(panel.shape, dtype), mask] + rest,
                                      [pltpu.SMEM((steps,), nonzero.dtype), pltpu.VMEM(panel.shape, dtype), inverse], 3,
                                      SOLVE, (nonzero[:, 0], panel, diag_inv), "solve_rest")
    far = len(cuts[-1])
    return factor, mask, slabs, [rests[:1]] + [rests[i:i + far] for i in range(1, len(rests), far)]


def pick_kernel(sources, *refs):
    ins, (keep, packed) = refs[:sources], refs[sources:]
    span = ins[0].shape[0]
    c, r = lax.axis_index("pcol"), lax.axis_index("prow")
    packed[span:] = ins[0][...]
    for k in range(sources):
        @pl.when(jnp.bitwise_xor(r, lax.rem(c, sources)) == k)
        def _():
            keep[...] = ins[k][...]

        @pl.when(jnp.bitwise_xor(r, lax.rem(jnp.bitwise_xor(c, 1), sources)) == k)
        def _():
            packed[:span] = ins[k][...]


def pick(slabs):
    span, *rest = slabs[0].shape
    outs = [jax.ShapeDtypeStruct(slabs[0].shape, slabs[0].dtype), jax.ShapeDtypeStruct((2 * span, *rest), slabs[0].dtype)]
    return small_call(functools.partial(pick_kernel, len(slabs)), outs, slabs, "pick")


def small_call(kernel, outs, args, name):
    return pl.pallas_call(
        kernel,
        out_shape=outs,
        in_specs=[VMEM] * len(args),
        out_specs=jax.tree.map(lambda _: VMEM, outs),
        cost_estimate=pl.CostEstimate(flops=0, bytes_accessed=1024, transcendentals=0),
        compiler_params=pltpu.CompilerParams(vmem_limit_bytes=SMALL),
        name=name,
    )(*args)


def choose_kernel(bit, mine, came, out):
    away = jnp.bitwise_xor(lax.axis_index("prow"), lax.rem(lax.axis_index("pcol"), lax.axis_size("prow")))
    here = jnp.bitwise_and(away, bit) == 0

    @pl.when(here)
    def _():
        out[...] = mine[...]

    @pl.when(jnp.logical_not(here))
    def _():
        out[...] = came[...]


def choose(bit, mine, came):
    shape = jax.ShapeDtypeStruct(mine.shape, mine.dtype)
    return small_call(functools.partial(choose_kernel, bit), shape, (mine, came), "choose")


def pack_kernel(mine, came, first, keep, packed):
    span = first.shape[0]
    here = lax.rem(lax.axis_index("prow"), 2) == lax.rem(lax.axis_index("pcol"), 2)
    packed[span:] = first[...]

    @pl.when(here)
    def _():
        keep[...] = mine[...]
        packed[:span] = came[...]

    @pl.when(jnp.logical_not(here))
    def _():
        keep[...] = came[...]
        packed[:span] = mine[...]


def pack(mine, came, first):
    span, *rest = first.shape
    outs = [jax.ShapeDtypeStruct(first.shape, first.dtype), jax.ShapeDtypeStruct((2 * span, *rest), first.dtype)]
    return small_call(pack_kernel, outs, (mine, came, first), "pack")


def join_kernel(*refs):
    at = 0
    for ref in refs[:-1]:
        refs[-1][at:at + ref.shape[0]] = ref[...]
        at += ref.shape[0]


def join(parts):
    total = sum(x.shape[0] for x in parts)
    return small_call(join_kernel, jax.ShapeDtypeStruct((total, *parts[0].shape[1:]), parts[0].dtype), parts, "join")


def masked_kernel(mask, *refs):
    for n, ref in enumerate(refs[:-1]):
        refs[-1][n] = (ref[0].astype(jnp.float32) * mask[...]).astype(ref.dtype)


def masked(mask, parts):
    shape = jax.ShapeDtypeStruct((len(parts), *parts[0].shape[1:]), parts[0].dtype)
    return small_call(masked_kernel, shape, (mask, *parts), "masked")


def hold_kernel(x, _, out):
    del x, out


def hold(x, until):
    return pl.pallas_call(
        hold_kernel,
        out_shape=jax.ShapeDtypeStruct(x.shape, x.dtype),
        in_specs=[HBM, HBM],
        out_specs=HBM,
        input_output_aliases={0: 0},
        cost_estimate=pl.CostEstimate(flops=0, bytes_accessed=1024, transcendentals=0),
        compiler_params=pltpu.CompilerParams(vmem_limit_bytes=SMALL),
        name="hold",
    )(x, until)


def renew_kernel(plan, chips, *refs):
    operands, (trailing, out, rows_full, column, held, out_sems) = refs[:len(plan)], refs[len(plan):]
    steps, size = held.shape[0], held.shape[1]
    rows = size // (2 * chips)
    c, r = lax.axis_index("pcol"), lax.axis_index("prow")
    grid_rows = lax.axis_size("prow")
    own = c // grid_rows
    order = [lax.rem(own + m, steps) for m in range(steps)]
    for ref, places in zip(operands, plan):
        for at, (m, core, k) in enumerate(places):
            source = jnp.bitwise_xor(c, 2 * k + core)
            here = pl.ds(pl.multiple_of(source * rows, rows), rows)
            if m is None:
                column[here] = ref[at]
            else:
                rows_full[m, here] = ref[at]
    for m in range(steps):
        product = lax.dot_general(rows_full[m], column[...], TRANSPOSED, preferred_element_type=jnp.float32)
        before = trailing[order[m], 0, 0, 0]
        renewed = (before.astype(jnp.float32) - product).astype(held.dtype)
        held[m] = jnp.where(order[m] * grid_rows + r >= c, renewed, before)
        pltpu.make_async_copy(held.at[m], out.at[order[m], 0, 0, 0], out_sems.at[m]).start()
    for m in range(steps):
        pltpu.make_async_copy(held.at[m], out.at[order[m], 0, 0, 0], out_sems.at[m]).wait()


def renew(trailing, chips, operands, plan):
    steps, size = trailing.shape[0], trailing.shape[-1]
    tiles = pltpu.VMEM((steps, size, size), trailing.dtype)
    args = (*operands, trailing)
    return pl.pallas_call(
        functools.partial(renew_kernel, plan, chips),
        out_shape=jax.ShapeDtypeStruct(trailing.shape, trailing.dtype),
        in_specs=[VMEM] * len(args),
        out_specs=HBM,
        scratch_shapes=[
            tiles,
            pltpu.VMEM((size, size), trailing.dtype),
            tiles,
            pltpu.SemaphoreType.DMA((steps,)),
        ],
        compiler_params=pltpu.CompilerParams(vmem_limit_bytes=LIMIT),
        name="renew",
    )(*args)


def body(panel, diag_inv, nonzero, trailing):
    grid_rows, grid_cols = lax.axis_size("prow"), lax.axis_size("pcol")
    chips = grid_cols // 2
    classes = max(1, grid_cols // grid_rows)
    steps = panel.shape[0]
    factor, mask, slabs, rests = solve(panel, diag_inv, nonzero, classes)
    slabs = list(slabs)

    def kind(k):
        return 2 * k // grid_rows

    def gather(parts, relay, ks, held):
        for k in ks:
            low = k & -k
            relayed = relay and low != k and kind(low) == 0
            source = held[k ^ low] if relayed else parts[kind(k)]
            held[k] = swap(source, "pcol", 2 * low if relayed else 2 * k)
        return held

    top = chips // 2
    near = gather(slabs, PREL, range(1, chips), {0: slabs[0]})
    half = max(1, chips // GROUPS)
    firsts = [masked(mask, [near[k] for k in range(n, n + half)]) for n in range(0, chips, half)]
    marks = {"p1": near[1], "p2": near[top], "p3": near[chips - 1], "b": firsts[-1], "a": firsts[0]}
    own_rest = rests[0][0]
    if G1:
        own_rest = hold(own_rest, marks[G1])
    close = [k for k in range(1, chips) if kind(k) == 0]
    far = [k for k in range(1, chips) if kind(k) != 0]
    rest = gather([own_rest], QREL, close, {0: own_rest})
    cuts = CUTS(steps)
    pieces = []
    for i in range(len(cuts)):
        parts = [None] + [row[i] for row in rests[1:]]
        if G2 and parts[1:]:
            parts[1] = hold(parts[1], marks[G2])
        pieces.append(gather(parts, QREL, far, {}))
    operands, plan = [], []

    def use(x, places):
        operands.append(x)
        plan.append(tuple(places))

    def both(x, places):
        use(x, [(m, 0, k) for m, k in places])
        use(swap(x, "pcol", 1), [(m, 1, k) for m, k in places])

    for n, first in enumerate(firsts):
        group = range(n * half, (n + 1) * half)
        if XY == "hyper":
            mine = first
            bit = grid_rows // 2
            while bit > 1:
                mine = choose(bit, mine, swap(mine, "prow", bit))
                bit //= 2
            if GX and n == GX[0]:
                mine = hold(mine, pieces[0][top])
            keep, packed = pack(mine, swap(mine, "prow", 1), first)
        else:
            keep, packed = pick([first] + [swap(first, "prow", k) for k in range(1, grid_rows)])
        use(keep, [(None, 0, k) for k in group])
        use(first, [(0, 0, k) for k in group])
        use(swap(packed, "pcol", 1), [(None, 1, k) for k in group] + [(0, 1, k) for k in group])
    joined = [0] + close
    both(join([rest[k] for k in joined]), [(m, k) for k in joined for m in range(1, steps)])
    for k in far:
        m = 1
        for i, cut in enumerate(cuts):
            both(pieces[i][k], [(m + j, k) for j in range(cut)])
            m += cut
    renewed = renew(trailing, chips, operands, plan)
    return factor, renewed


GX = (1,)


PREL = True
QREL = True
GROUPS = 2
G1 = None
G2 = None
XY = 'hyper'


def CUTS(steps):
    return [steps - 1]


def solution(mesh):
    placed = (
        P(None, "prow", "pcol", None),
        P(),
        P(None, "prow"),
        P(None, "prow", None, "pcol", None, None),
    )
    return jax.shard_map(
        body,
        mesh=mesh,
        in_specs=placed,
        out_specs=(P(None, "prow", "pcol", None), P(None, "prow", None, "pcol", None, None)),
        check_vma=False,
    )
```

```python
import functools

import jax
import jax.numpy as jnp
from jax import lax
from jax.experimental import pallas as pl
from jax.experimental.pallas import tpu as pltpu
from jax.sharding import PartitionSpec as P

TRANSPOSED = (((1,), (1,)), ((), ()))
HBM = pl.BlockSpec(memory_space=pl.ANY)
VMEM = pl.BlockSpec(memory_space=pltpu.VMEM)
SMEM = pl.BlockSpec(memory_space=pltpu.SMEM)
LIMIT = 16 * 1024 * 1024
FIRST = 56418304
SOLVE = 56152064
SMALL = 8 * 1024 * 1024


def swap(x, axis, distance):
    size = lax.axis_size(axis)
    return lax.ppermute(x, axis, [(i, i ^ distance) for i in range(size)])


def load(pairs, sems):
    copies = [pltpu.make_async_copy(*pair, sems.at[n]) for n, pair in enumerate(pairs)]
    for copy in copies:
        copy.start()
    for copy in copies:
        copy.wait()


def first_kernel(classes, panel, diag_inv, *refs):
    slabs, (strips, inverse, sems) = refs[:classes], refs[classes:]
    own = lax.axis_index("pcol") // lax.axis_size("prow")
    load([(diag_inv, inverse)]
         + [(panel.at[jnp.bitwise_xor(own, n), 0], strips.at[n]) for n in range(classes)], sems)
    rows, size = strips.shape[1:]
    product = lax.dot_general(strips[...].reshape(classes * rows, size), inverse[...], TRANSPOSED,
                              preferred_element_type=jnp.float32).reshape(classes, rows, size)
    for n in range(classes):
        slabs[n][0] = product[n].astype(strips.dtype)


def rest_kernel(classes, nonzero, panel, diag_inv, _, mask, *refs):
    rests, (live, strips, inverse, sems) = refs[:-4], refs[-4:]
    load([(nonzero, live), (panel, strips), (diag_inv, inverse)], sems)
    steps, _, rows, size = strips.shape
    product = lax.dot_general(strips[...].reshape(steps * rows, size), inverse[...], TRANSPOSED,
                              preferred_element_type=jnp.float32).reshape(steps, rows, size)
    for s in range(steps):
        strips[s, 0] = (product[s] * live[s].astype(jnp.float32)).astype(strips.dtype)
    own = lax.axis_index("pcol") // lax.axis_size("prow")
    mask[...] = jnp.full(mask.shape, live[own].astype(jnp.float32), mask.dtype)
    for n in range(classes):
        for m in range(1, steps):
            rests[n][m - 1] = strips[lax.rem(jnp.bitwise_xor(own, n) + m, steps), 0]


def solve_call(kernel, outs, scratch, copies, limit, args, name, inputs):
    return pl.pallas_call(
        kernel,
        out_shape=outs,
        in_specs=[pl.BlockSpec(memory_space=pltpu.HBM)] * inputs + [VMEM] * (len(args) - inputs),
        out_specs=[VMEM] * len(outs),
        scratch_shapes=scratch + [pltpu.SemaphoreType.DMA((copies,))],
        cost_estimate=pl.CostEstimate(flops=0, bytes_accessed=1024, transcendentals=0),
        compiler_params=pltpu.CompilerParams(vmem_limit_bytes=limit),
        name=name,
    )(*args)


def solve(panel, diag_inv, nonzero, classes):
    steps, _, rows, size = panel.shape
    dtype = panel.dtype
    slab = jax.ShapeDtypeStruct((1, rows, size), dtype)
    cuts = [[steps - 1]] + [CUTS(steps)] * (classes - 1)
    rest = [jax.ShapeDtypeStruct((n, rows, size), dtype) for cut in cuts for n in cut]
    mask = jax.ShapeDtypeStruct((1, size), jnp.float32)
    inverse = pltpu.VMEM(diag_inv.shape, dtype)
    slabs = solve_call(functools.partial(first_kernel, classes), [slab] * classes,
                       [pltpu.VMEM((classes, rows, size), dtype), inverse], 1 + classes, FIRST,
                       (panel, diag_inv), "solve_first", 2)
    mask, *rests = solve_call(functools.partial(rest_kernel, classes), [mask] + rest,
                              [pltpu.SMEM((steps,), nonzero.dtype), pltpu.VMEM(panel.shape, dtype), inverse], 3,
                              SOLVE, (nonzero[:, 0], panel, diag_inv, slabs[0]), "solve_rest", 3)
    return mask, slabs, [[x] for x in rests]


def pick_kernel(sources, *refs):
    ins, (keep, packed) = refs[:sources], refs[sources:]
    span = ins[0].shape[0]
    c, r = lax.axis_index("pcol"), lax.axis_index("prow")
    packed[span:] = ins[0][...]
    for k in range(sources):
        @pl.when(jnp.bitwise_xor(r, lax.rem(c, sources)) == k)
        def _():
            keep[...] = ins[k][...]

        @pl.when(jnp.bitwise_xor(r, lax.rem(jnp.bitwise_xor(c, 1), sources)) == k)
        def _():
            packed[:span] = ins[k][...]


def pick(slabs):
    span, *rest = slabs[0].shape
    outs = [jax.ShapeDtypeStruct(slabs[0].shape, slabs[0].dtype), jax.ShapeDtypeStruct((2 * span, *rest), slabs[0].dtype)]
    return small_call(functools.partial(pick_kernel, len(slabs)), outs, slabs, "pick")


def small_call(kernel, outs, args, name):
    return pl.pallas_call(
        kernel,
        out_shape=outs,
        in_specs=[VMEM] * len(args),
        out_specs=jax.tree.map(lambda _: VMEM, outs),
        cost_estimate=pl.CostEstimate(flops=0, bytes_accessed=1024, transcendentals=0),
        compiler_params=pltpu.CompilerParams(vmem_limit_bytes=SMALL),
        name=name,
    )(*args)


def choose_kernel(bit, mine, came, out):
    away = jnp.bitwise_xor(lax.axis_index("prow"), lax.rem(lax.axis_index("pcol"), lax.axis_size("prow")))
    here = jnp.bitwise_and(away, bit) == 0

    @pl.when(here)
    def _():
        out[...] = mine[...]

    @pl.when(jnp.logical_not(here))
    def _():
        out[...] = came[...]


def choose(bit, mine, came):
    shape = jax.ShapeDtypeStruct(mine.shape, mine.dtype)
    return small_call(functools.partial(choose_kernel, bit), shape, (mine, came), "choose")


def pack_kernel(mine, came, first, keep, packed):
    span = first.shape[0]
    here = lax.rem(lax.axis_index("prow"), 2) == lax.rem(lax.axis_index("pcol"), 2)
    packed[span:] = first[...]

    @pl.when(here)
    def _():
        keep[...] = mine[...]
        packed[:span] = came[...]

    @pl.when(jnp.logical_not(here))
    def _():
        keep[...] = came[...]
        packed[:span] = mine[...]


def pack(mine, came, first):
    span, *rest = first.shape
    outs = [jax.ShapeDtypeStruct(first.shape, first.dtype), jax.ShapeDtypeStruct((2 * span, *rest), first.dtype)]
    return small_call(pack_kernel, outs, (mine, came, first), "pack")


def join_kernel(*refs):
    at = 0
    for ref in refs[:-1]:
        refs[-1][at:at + ref.shape[0]] = ref[...]
        at += ref.shape[0]


def join(parts):
    total = sum(x.shape[0] for x in parts)
    return small_call(join_kernel, jax.ShapeDtypeStruct((total, *parts[0].shape[1:]), parts[0].dtype), parts, "join")


def masked_kernel(mask, *refs):
    for n, ref in enumerate(refs[:-1]):
        refs[-1][n] = (ref[0].astype(jnp.float32) * mask[...]).astype(ref.dtype)


def masked(mask, parts):
    shape = jax.ShapeDtypeStruct((len(parts), *parts[0].shape[1:]), parts[0].dtype)
    return small_call(masked_kernel, shape, (mask, *parts), "masked")


def finish_kernel(first, *refs):
    pair, factor = refs[-2:]
    join_kernel(*refs[:-1])
    steps = factor.shape[0]
    own = lax.axis_index("pcol") // lax.axis_size("prow")
    factor[own, 0] = first[0]
    for m in range(1, steps):
        factor[lax.rem(own + m, steps), 0] = refs[0][m - 1]


def finish(first, parts):
    total = sum(x.shape[0] for x in parts)
    steps, rows, size = parts[0].shape[0] + 1, *parts[0].shape[1:]
    outs = [jax.ShapeDtypeStruct((total, rows, size), first.dtype),
            jax.ShapeDtypeStruct((steps, 1, rows, size), first.dtype)]
    return small_call(finish_kernel, outs, (first, *parts), "finish")


def hold_kernel(x, _, out):
    del x, out


def hold(x, until):
    return pl.pallas_call(
        hold_kernel,
        out_shape=jax.ShapeDtypeStruct(x.shape, x.dtype),
        in_specs=[HBM, HBM],
        out_specs=HBM,
        input_output_aliases={0: 0},
        cost_estimate=pl.CostEstimate(flops=0, bytes_accessed=1024, transcendentals=0),
        compiler_params=pltpu.CompilerParams(vmem_limit_bytes=SMALL),
        name="hold",
    )(x, until)


def renew_kernel(plan, chips, *refs):
    operands, (trailing, out, rows_full, column, held, out_sems) = refs[:len(plan)], refs[len(plan):]
    steps, size = held.shape[0], held.shape[1]
    rows = size // (2 * chips)
    c, r = lax.axis_index("pcol"), lax.axis_index("prow")
    grid_rows = lax.axis_size("prow")
    own = c // grid_rows
    order = [lax.rem(own + m, steps) for m in range(steps)]
    for ref, places in zip(operands, plan):
        for at, (m, core, k) in enumerate(places):
            source = jnp.bitwise_xor(c, 2 * k + core)
            here = pl.ds(pl.multiple_of(source * rows, rows), rows)
            if m is None:
                column[here] = ref[at]
            else:
                rows_full[m, here] = ref[at]
    for m in range(steps):
        product = lax.dot_general(rows_full[m], column[...], TRANSPOSED, preferred_element_type=jnp.float32)
        before = trailing[order[m], 0, 0, 0]
        renewed = (before.astype(jnp.float32) - product).astype(held.dtype)
        held[m] = jnp.where(order[m] * grid_rows + r >= c, renewed, before)
        pltpu.make_async_copy(held.at[m], out.at[order[m], 0, 0, 0], out_sems.at[m]).start()
    for m in range(steps):
        pltpu.make_async_copy(held.at[m], out.at[order[m], 0, 0, 0], out_sems.at[m]).wait()


def renew(trailing, chips, operands, plan):
    steps, size = trailing.shape[0], trailing.shape[-1]
    tiles = pltpu.VMEM((steps, size, size), trailing.dtype)
    args = (*operands, trailing)
    return pl.pallas_call(
        functools.partial(renew_kernel, plan, chips),
        out_shape=jax.ShapeDtypeStruct(trailing.shape, trailing.dtype),
        in_specs=[VMEM] * len(args),
        out_specs=HBM,
        scratch_shapes=[
            tiles,
            pltpu.VMEM((size, size), trailing.dtype),
            tiles,
            pltpu.SemaphoreType.DMA((steps,)),
        ],
        compiler_params=pltpu.CompilerParams(vmem_limit_bytes=LIMIT),
        name="renew",
    )(*args)


def body(panel, diag_inv, nonzero, trailing):
    grid_rows, grid_cols = lax.axis_size("prow"), lax.axis_size("pcol")
    chips = grid_cols // 2
    classes = max(1, grid_cols // grid_rows)
    steps = panel.shape[0]
    mask, slabs, rests = solve(panel, diag_inv, nonzero, classes)
    slabs = list(slabs)

    def kind(k):
        return 2 * k // grid_rows

    def gather(parts, relay, ks, held):
        for k in ks:
            low = k & -k
            relayed = relay and low != k and kind(low) == 0
            source = held[k ^ low] if relayed else parts[kind(k)]
            held[k] = swap(source, "pcol", 2 * low if relayed else 2 * k)
        return held

    top = chips // 2
    near = gather(slabs, PREL, range(1, chips), {0: slabs[0]})
    half = max(1, chips // GROUPS)
    firsts = [masked(mask, [near[k] for k in range(n, n + half)]) for n in range(0, chips, half)]
    marks = {"p1": near[1], "p2": near[top], "p3": near[chips - 1], "b": firsts[-1], "a": firsts[0]}
    own_rest = rests[0][0]
    if G1:
        own_rest = hold(own_rest, marks[G1])
    close = [k for k in range(1, chips) if kind(k) == 0]
    far = [k for k in range(1, chips) if kind(k) != 0]
    rest = gather([own_rest], QREL, close, {0: own_rest})
    cuts = CUTS(steps)
    pieces = []
    for i in range(len(cuts)):
        parts = [None] + [row[i] for row in rests[1:]]
        if G2 and parts[1:]:
            parts[1] = hold(parts[1], marks[G2])
        pieces.append(gather(parts, QREL, far, {}))
    operands, plan = [], []

    def use(x, places):
        operands.append(x)
        plan.append(tuple(places))

    def both(x, places):
        use(x, [(m, 0, k) for m, k in places])
        use(swap(x, "pcol", 1), [(m, 1, k) for m, k in places])

    for n, first in enumerate(firsts):
        group = range(n * half, (n + 1) * half)
        if XY == "hyper":
            mine = first
            bit = grid_rows // 2
            while bit > 1:
                mine = choose(bit, mine, swap(mine, "prow", bit))
                bit //= 2
            if GX and n == GX[0]:
                mine = hold(mine, pieces[0][top])
            keep, packed = pack(mine, swap(mine, "prow", 1), first)
        else:
            keep, packed = pick([first] + [swap(first, "prow", k) for k in range(1, grid_rows)])
        use(keep, [(None, 0, k) for k in group])
        use(first, [(0, 0, k) for k in group])
        use(swap(packed, "pcol", 1), [(None, 1, k) for k in group] + [(0, 1, k) for k in group])
    joined = [0] + close
    pair, factor = finish(firsts[0], [rest[k] for k in joined])
    both(pair, [(m, k) for k in joined for m in range(1, steps)])
    for k in far:
        m = 1
        for i, cut in enumerate(cuts):
            both(pieces[i][k], [(m + j, k) for j in range(cut)])
            m += cut
    renewed = renew(trailing, chips, operands, plan)
    return factor, renewed


GX = None


PREL = False
QREL = True
GROUPS = 2
G1 = 'a'
G2 = None
XY = 'hyper'


def CUTS(steps):
    return [steps - 1]


def solution(mesh):
    placed = (
        P(None, "prow", "pcol", None),
        P(),
        P(None, "prow"),
        P(None, "prow", None, "pcol", None, None),
    )
    return jax.shard_map(
        body,
        mesh=mesh,
        in_specs=placed,
        out_specs=(P(None, "prow", "pcol", None), P(None, "prow", None, "pcol", None, None)),
        check_vma=False,
    )
```

```python
import functools

import jax
import jax.numpy as jnp
from jax import lax
from jax.experimental import pallas as pl
from jax.experimental.pallas import tpu as pltpu
from jax.sharding import PartitionSpec as P

TRANSPOSED = (((1,), (1,)), ((), ()))
HBM = pl.BlockSpec(memory_space=pl.ANY)
VMEM = pl.BlockSpec(memory_space=pltpu.VMEM)
SMEM = pl.BlockSpec(memory_space=pltpu.SMEM)
LIMIT = 16 * 1024 * 1024
FIRST = 56418304
SOLVE = 56152064
SMALL = 8 * 1024 * 1024


def swap(x, axis, distance):
    size = lax.axis_size(axis)
    return lax.ppermute(x, axis, [(i, i ^ distance) for i in range(size)])


def load(pairs, sems):
    copies = [pltpu.make_async_copy(*pair, sems.at[n]) for n, pair in enumerate(pairs)]
    for copy in copies:
        copy.start()
    for copy in copies:
        copy.wait()


def first_kernel(classes, panel, diag_inv, *refs):
    slabs, (strips, inverse, sems) = refs[:classes], refs[classes:]
    own = lax.axis_index("pcol") // lax.axis_size("prow")
    load([(diag_inv, inverse)]
         + [(panel.at[jnp.bitwise_xor(own, n), 0], strips.at[n]) for n in range(classes)], sems)
    rows, size = strips.shape[1:]
    product = lax.dot_general(strips[...].reshape(classes * rows, size), inverse[...], TRANSPOSED,
                              preferred_element_type=jnp.float32).reshape(classes, rows, size)
    for n in range(classes):
        slabs[n][0] = product[n].astype(strips.dtype)


def rest_kernel(classes, nonzero, panel, diag_inv, mask, *refs):
    rests, (live, strips, inverse, sems) = refs[:-4], refs[-4:]
    load([(nonzero, live), (panel, strips), (diag_inv, inverse)], sems)
    steps, _, rows, size = strips.shape
    product = lax.dot_general(strips[...].reshape(steps * rows, size), inverse[...], TRANSPOSED,
                              preferred_element_type=jnp.float32).reshape(steps, rows, size)
    for s in range(steps):
        strips[s, 0] = (product[s] * live[s].astype(jnp.float32)).astype(strips.dtype)
    own = lax.axis_index("pcol") // lax.axis_size("prow")
    mask[...] = jnp.full(mask.shape, live[own].astype(jnp.float32), mask.dtype)
    for n in range(classes):
        for m in range(1, steps):
            rests[n][m - 1] = strips[lax.rem(jnp.bitwise_xor(own, n) + m, steps), 0]


def solve_call(kernel, outs, scratch, copies, limit, args, name):
    return pl.pallas_call(
        kernel,
        out_shape=outs,
        in_specs=[pl.BlockSpec(memory_space=pltpu.HBM)] * len(args),
        out_specs=[VMEM] * len(outs),
        scratch_shapes=scratch + [pltpu.SemaphoreType.DMA((copies,))],
        cost_estimate=pl.CostEstimate(flops=0, bytes_accessed=1024, transcendentals=0),
        compiler_params=pltpu.CompilerParams(vmem_limit_bytes=limit),
        name=name,
    )(*args)


def solve(panel, diag_inv, nonzero, classes):
    steps, _, rows, size = panel.shape
    dtype = panel.dtype
    slab = jax.ShapeDtypeStruct((1, rows, size), dtype)
    cuts = [[steps - 1]] + [CUTS(steps)] * (classes - 1)
    rest = [jax.ShapeDtypeStruct((n, rows, size), dtype) for cut in cuts for n in cut]
    mask = jax.ShapeDtypeStruct((1, size), jnp.float32)
    inverse = pltpu.VMEM(diag_inv.shape, dtype)
    slabs = solve_call(functools.partial(first_kernel, classes), [slab] * classes,
                       [pltpu.VMEM((classes, rows, size), dtype), inverse], 1 + classes, FIRST,
                       (panel, diag_inv), "solve_first")
    mask, *rests = solve_call(functools.partial(rest_kernel, classes), [mask] + rest,
                              [pltpu.SMEM((steps,), nonzero.dtype), pltpu.VMEM(panel.shape, dtype), inverse], 3,
                              SOLVE, (nonzero[:, 0], panel, diag_inv), "solve_rest")
    return mask, slabs, [[x] for x in rests]


def pick_kernel(sources, *refs):
    ins, (keep, packed) = refs[:sources], refs[sources:]
    span = ins[0].shape[0]
    c, r = lax.axis_index("pcol"), lax.axis_index("prow")
    packed[span:] = ins[0][...]
    for k in range(sources):
        @pl.when(jnp.bitwise_xor(r, lax.rem(c, sources)) == k)
        def _():
            keep[...] = ins[k][...]

        @pl.when(jnp.bitwise_xor(r, lax.rem(jnp.bitwise_xor(c, 1), sources)) == k)
        def _():
            packed[:span] = ins[k][...]


def pick(slabs):
    span, *rest = slabs[0].shape
    outs = [jax.ShapeDtypeStruct(slabs[0].shape, slabs[0].dtype), jax.ShapeDtypeStruct((2 * span, *rest), slabs[0].dtype)]
    return small_call(functools.partial(pick_kernel, len(slabs)), outs, slabs, "pick")


def small_call(kernel, outs, args, name):
    return pl.pallas_call(
        kernel,
        out_shape=outs,
        in_specs=[VMEM] * len(args),
        out_specs=jax.tree.map(lambda _: VMEM, outs),
        cost_estimate=pl.CostEstimate(flops=0, bytes_accessed=1024, transcendentals=0),
        compiler_params=pltpu.CompilerParams(vmem_limit_bytes=SMALL),
        name=name,
    )(*args)


def choose_kernel(bit, mine, came, out):
    away = jnp.bitwise_xor(lax.axis_index("prow"), lax.rem(lax.axis_index("pcol"), lax.axis_size("prow")))
    here = jnp.bitwise_and(away, bit) == 0

    @pl.when(here)
    def _():
        out[...] = mine[...]

    @pl.when(jnp.logical_not(here))
    def _():
        out[...] = came[...]


def choose(bit, mine, came):
    shape = jax.ShapeDtypeStruct(mine.shape, mine.dtype)
    return small_call(functools.partial(choose_kernel, bit), shape, (mine, came), "choose")


def pack_kernel(mine, came, first, keep, packed):
    span = first.shape[0]
    here = lax.rem(lax.axis_index("prow"), 2) == lax.rem(lax.axis_index("pcol"), 2)
    packed[span:] = first[...]

    @pl.when(here)
    def _():
        keep[...] = mine[...]
        packed[:span] = came[...]

    @pl.when(jnp.logical_not(here))
    def _():
        keep[...] = came[...]
        packed[:span] = mine[...]


def pack(mine, came, first):
    span, *rest = first.shape
    outs = [jax.ShapeDtypeStruct(first.shape, first.dtype), jax.ShapeDtypeStruct((2 * span, *rest), first.dtype)]
    return small_call(pack_kernel, outs, (mine, came, first), "pack")


def join_kernel(*refs):
    at = 0
    for ref in refs[:-1]:
        refs[-1][at:at + ref.shape[0]] = ref[...]
        at += ref.shape[0]


def join(parts):
    total = sum(x.shape[0] for x in parts)
    return small_call(join_kernel, jax.ShapeDtypeStruct((total, *parts[0].shape[1:]), parts[0].dtype), parts, "join")


def masked_kernel(mask, *refs):
    for n, ref in enumerate(refs[:-1]):
        refs[-1][n] = (ref[0].astype(jnp.float32) * mask[...]).astype(ref.dtype)


def masked(mask, parts):
    shape = jax.ShapeDtypeStruct((len(parts), *parts[0].shape[1:]), parts[0].dtype)
    return small_call(masked_kernel, shape, (mask, *parts), "masked")


def finish_kernel(first, *refs):
    pair, factor = refs[-2:]
    join_kernel(*refs[:-1])
    steps = factor.shape[0]
    own = lax.axis_index("pcol") // lax.axis_size("prow")
    factor[own, 0] = first[0]
    for m in range(1, steps):
        factor[lax.rem(own + m, steps), 0] = refs[0][m - 1]


def finish(first, parts):
    total = sum(x.shape[0] for x in parts)
    steps, rows, size = parts[0].shape[0] + 1, *parts[0].shape[1:]
    outs = [jax.ShapeDtypeStruct((total, rows, size), first.dtype),
            jax.ShapeDtypeStruct((steps, 1, rows, size), first.dtype)]
    return small_call(finish_kernel, outs, (first, *parts), "finish")


def hold_kernel(x, _, out):
    del x, out


def hold(x, until):
    return pl.pallas_call(
        hold_kernel,
        out_shape=jax.ShapeDtypeStruct(x.shape, x.dtype),
        in_specs=[HBM, HBM],
        out_specs=HBM,
        input_output_aliases={0: 0},
        cost_estimate=pl.CostEstimate(flops=0, bytes_accessed=1024, transcendentals=0),
        compiler_params=pltpu.CompilerParams(vmem_limit_bytes=SMALL),
        name="hold",
    )(x, until)


def renew_kernel(plan, chips, *refs):
    operands, (trailing, out, rows_full, column, held, out_sems) = refs[:len(plan)], refs[len(plan):]
    steps, size = held.shape[0], held.shape[1]
    rows = size // (2 * chips)
    c, r = lax.axis_index("pcol"), lax.axis_index("prow")
    grid_rows = lax.axis_size("prow")
    own = c // grid_rows
    order = [lax.rem(own + m, steps) for m in range(steps)]
    for ref, places in zip(operands, plan):
        for at, (m, core, k) in enumerate(places):
            source = jnp.bitwise_xor(c, 2 * k + core)
            here = pl.ds(pl.multiple_of(source * rows, rows), rows)
            if m is None:
                column[here] = ref[at]
            else:
                rows_full[m, here] = ref[at]
    for m in range(steps):
        product = lax.dot_general(rows_full[m], column[...], TRANSPOSED, preferred_element_type=jnp.float32)
        before = trailing[order[m], 0, 0, 0]
        renewed = (before.astype(jnp.float32) - product).astype(held.dtype)
        held[m] = jnp.where(order[m] * grid_rows + r >= c, renewed, before)
        pltpu.make_async_copy(held.at[m], out.at[order[m], 0, 0, 0], out_sems.at[m]).start()
    for m in range(steps):
        pltpu.make_async_copy(held.at[m], out.at[order[m], 0, 0, 0], out_sems.at[m]).wait()


def renew(trailing, chips, operands, plan):
    steps, size = trailing.shape[0], trailing.shape[-1]
    tiles = pltpu.VMEM((steps, size, size), trailing.dtype)
    args = (*operands, trailing)
    return pl.pallas_call(
        functools.partial(renew_kernel, plan, chips),
        out_shape=jax.ShapeDtypeStruct(trailing.shape, trailing.dtype),
        in_specs=[VMEM] * len(args),
        out_specs=HBM,
        scratch_shapes=[
            tiles,
            pltpu.VMEM((size, size), trailing.dtype),
            tiles,
            pltpu.SemaphoreType.DMA((steps,)),
        ],
        compiler_params=pltpu.CompilerParams(vmem_limit_bytes=LIMIT),
        name="renew",
    )(*args)


def body(panel, diag_inv, nonzero, trailing):
    grid_rows, grid_cols = lax.axis_size("prow"), lax.axis_size("pcol")
    chips = grid_cols // 2
    classes = max(1, grid_cols // grid_rows)
    steps = panel.shape[0]
    mask, slabs, rests = solve(panel, diag_inv, nonzero, classes)
    slabs = list(slabs)

    def kind(k):
        return 2 * k // grid_rows

    def gather(parts, relay, ks, held):
        for k in ks:
            low = k & -k
            relayed = relay and low != k and kind(low) == 0
            source = held[k ^ low] if relayed else parts[kind(k)]
            held[k] = swap(source, "pcol", 2 * low if relayed else 2 * k)
        return held

    top = chips // 2
    near = gather(slabs, PREL, range(1, chips), {0: slabs[0]})
    half = max(1, chips // GROUPS)
    firsts = [masked(mask, [near[k] for k in range(n, n + half)]) for n in range(0, chips, half)]
    marks = {"p1": near[1], "p2": near[top], "p3": near[chips - 1], "b": firsts[-1], "a": firsts[0]}
    own_rest = rests[0][0]
    if G1:
        own_rest = hold(own_rest, marks[G1])
    close = [k for k in range(1, chips) if kind(k) == 0]
    far = [k for k in range(1, chips) if kind(k) != 0]
    rest = gather([own_rest], QREL, close, {0: own_rest})
    cuts = CUTS(steps)
    pieces = []
    for i in range(len(cuts)):
        parts = [None] + [row[i] for row in rests[1:]]
        if G2 and parts[1:]:
            parts[1] = hold(parts[1], marks[G2])
        pieces.append(gather(parts, QREL, far, {}))
    operands, plan = [], []

    def use(x, places):
        operands.append(x)
        plan.append(tuple(places))

    def both(x, places):
        use(x, [(m, 0, k) for m, k in places])
        use(swap(x, "pcol", 1), [(m, 1, k) for m, k in places])

    for n, first in enumerate(firsts):
        group = range(n * half, (n + 1) * half)
        if XY == "hyper":
            mine = first
            bit = grid_rows // 2
            while bit > 1:
                mine = choose(bit, mine, swap(mine, "prow", bit))
                bit //= 2
            if GX and n == GX[0]:
                mine = hold(mine, pieces[0][top])
            keep, packed = pack(mine, swap(mine, "prow", 1), first)
        else:
            keep, packed = pick([first] + [swap(first, "prow", k) for k in range(1, grid_rows)])
        use(keep, [(None, 0, k) for k in group])
        use(first, [(0, 0, k) for k in group])
        use(swap(packed, "pcol", 1), [(None, 1, k) for k in group] + [(0, 1, k) for k in group])
    joined = [0] + close
    pair, factor = finish(firsts[0], [rest[k] for k in joined])
    both(pair, [(m, k) for k in joined for m in range(1, steps)])
    for k in far:
        m = 1
        for i, cut in enumerate(cuts):
            both(pieces[i][k], [(m + j, k) for j in range(cut)])
            m += cut
    renewed = renew(trailing, chips, operands, plan)
    return factor, renewed


GX = None


PREL = False
QREL = True
GROUPS = 2
G1 = 'b'
G2 = None
XY = 'hyper'


def CUTS(steps):
    return [steps - 1]


def solution(mesh):
    placed = (
        P(None, "prow", "pcol", None),
        P(),
        P(None, "prow"),
        P(None, "prow", None, "pcol", None, None),
    )
    return jax.shard_map(
        body,
        mesh=mesh,
        in_specs=placed,
        out_specs=(P(None, "prow", "pcol", None), P(None, "prow", None, "pcol", None, None)),
        check_vma=False,
    )
```

```python
import functools

import jax
import jax.numpy as jnp
from jax import lax
from jax.experimental import pallas as pl
from jax.experimental.pallas import tpu as pltpu
from jax.sharding import PartitionSpec as P

TRANSPOSED = (((1,), (1,)), ((), ()))
HBM = pl.BlockSpec(memory_space=pl.ANY)
VMEM = pl.BlockSpec(memory_space=pltpu.VMEM)
SMEM = pl.BlockSpec(memory_space=pltpu.SMEM)
LIMIT = 16 * 1024 * 1024
FIRST = 56418304
SOLVE = 56152064
SMALL = 8 * 1024 * 1024


def swap(x, axis, distance):
    size = lax.axis_size(axis)
    return lax.ppermute(x, axis, [(i, i ^ distance) for i in range(size)])


def load(pairs, sems):
    copies = [pltpu.make_async_copy(*pair, sems.at[n]) for n, pair in enumerate(pairs)]
    for copy in copies:
        copy.start()
    for copy in copies:
        copy.wait()


def first_kernel(classes, panel, diag_inv, *refs):
    slabs, (strips, inverse, sems) = refs[:classes], refs[classes:]
    own = lax.axis_index("pcol") // lax.axis_size("prow")
    load([(diag_inv, inverse)]
         + [(panel.at[jnp.bitwise_xor(own, n), 0], strips.at[n]) for n in range(classes)], sems)
    rows, size = strips.shape[1:]
    product = lax.dot_general(strips[...].reshape(classes * rows, size), inverse[...], TRANSPOSED,
                              preferred_element_type=jnp.float32).reshape(classes, rows, size)
    for n in range(classes):
        slabs[n][0] = product[n].astype(strips.dtype)


def rest_kernel(classes, nonzero, panel, diag_inv, mask, *refs):
    rests, (live, strips, inverse, sems) = refs[:-4], refs[-4:]
    load([(nonzero, live), (panel, strips), (diag_inv, inverse)], sems)
    steps, _, rows, size = strips.shape
    product = lax.dot_general(strips[...].reshape(steps * rows, size), inverse[...], TRANSPOSED,
                              preferred_element_type=jnp.float32).reshape(steps, rows, size)
    for s in range(steps):
        strips[s, 0] = (product[s] * live[s].astype(jnp.float32)).astype(strips.dtype)
    own = lax.axis_index("pcol") // lax.axis_size("prow")
    mask[...] = jnp.full(mask.shape, live[own].astype(jnp.float32), mask.dtype)
    for n in range(classes):
        for m in range(1, steps):
            rests[n][m - 1] = strips[lax.rem(jnp.bitwise_xor(own, n) + m, steps), 0]


def solve_call(kernel, outs, scratch, copies, limit, args, name):
    return pl.pallas_call(
        kernel,
        out_shape=outs,
        in_specs=[pl.BlockSpec(memory_space=pltpu.HBM)] * len(args),
        out_specs=[VMEM] * len(outs),
        scratch_shapes=scratch + [pltpu.SemaphoreType.DMA((copies,))],
        cost_estimate=pl.CostEstimate(flops=0, bytes_accessed=1024, transcendentals=0),
        compiler_params=pltpu.CompilerParams(vmem_limit_bytes=limit),
        name=name,
    )(*args)


def solve(panel, diag_inv, nonzero, classes):
    steps, _, rows, size = panel.shape
    dtype = panel.dtype
    slab = jax.ShapeDtypeStruct((1, rows, size), dtype)
    cuts = [[steps - 1]] + [CUTS(steps)] * (classes - 1)
    rest = [jax.ShapeDtypeStruct((n, rows, size), dtype) for cut in cuts for n in cut]
    mask = jax.ShapeDtypeStruct((1, size), jnp.float32)
    inverse = pltpu.VMEM(diag_inv.shape, dtype)
    slabs = solve_call(functools.partial(first_kernel, classes), [slab] * classes,
                       [pltpu.VMEM((classes, rows, size), dtype), inverse], 1 + classes, FIRST,
                       (panel, diag_inv), "solve_first")
    mask, *rests = solve_call(functools.partial(rest_kernel, classes), [mask] + rest,
                              [pltpu.SMEM((steps,), nonzero.dtype), pltpu.VMEM(panel.shape, dtype), inverse], 3,
                              SOLVE, (nonzero[:, 0], panel, diag_inv), "solve_rest")
    return mask, slabs, [[x] for x in rests]


def pick_kernel(sources, *refs):
    ins, (keep, packed) = refs[:sources], refs[sources:]
    span = ins[0].shape[0]
    c, r = lax.axis_index("pcol"), lax.axis_index("prow")
    packed[span:] = ins[0][...]
    for k in range(sources):
        @pl.when(jnp.bitwise_xor(r, lax.rem(c, sources)) == k)
        def _():
            keep[...] = ins[k][...]

        @pl.when(jnp.bitwise_xor(r, lax.rem(jnp.bitwise_xor(c, 1), sources)) == k)
        def _():
            packed[:span] = ins[k][...]


def pick(slabs):
    span, *rest = slabs[0].shape
    outs = [jax.ShapeDtypeStruct(slabs[0].shape, slabs[0].dtype), jax.ShapeDtypeStruct((2 * span, *rest), slabs[0].dtype)]
    return small_call(functools.partial(pick_kernel, len(slabs)), outs, slabs, "pick")


def small_call(kernel, outs, args, name):
    return pl.pallas_call(
        kernel,
        out_shape=outs,
        in_specs=[VMEM] * len(args),
        out_specs=jax.tree.map(lambda _: VMEM, outs),
        cost_estimate=pl.CostEstimate(flops=0, bytes_accessed=1024, transcendentals=0),
        compiler_params=pltpu.CompilerParams(vmem_limit_bytes=SMALL),
        name=name,
    )(*args)


def choose_kernel(bit, mine, came, out):
    away = jnp.bitwise_xor(lax.axis_index("prow"), lax.rem(lax.axis_index("pcol"), lax.axis_size("prow")))
    here = jnp.bitwise_and(away, bit) == 0

    @pl.when(here)
    def _():
        out[...] = mine[...]

    @pl.when(jnp.logical_not(here))
    def _():
        out[...] = came[...]


def choose(bit, mine, came):
    shape = jax.ShapeDtypeStruct(mine.shape, mine.dtype)
    return small_call(functools.partial(choose_kernel, bit), shape, (mine, came), "choose")


def pack_kernel(mine, came, first, keep, packed):
    span = first.shape[0]
    here = lax.rem(lax.axis_index("prow"), 2) == lax.rem(lax.axis_index("pcol"), 2)
    packed[span:] = first[...]

    @pl.when(here)
    def _():
        keep[...] = mine[...]
        packed[:span] = came[...]

    @pl.when(jnp.logical_not(here))
    def _():
        keep[...] = came[...]
        packed[:span] = mine[...]


def pack(mine, came, first):
    span, *rest = first.shape
    outs = [jax.ShapeDtypeStruct(first.shape, first.dtype), jax.ShapeDtypeStruct((2 * span, *rest), first.dtype)]
    return small_call(pack_kernel, outs, (mine, came, first), "pack")


def join_kernel(*refs):
    at = 0
    for ref in refs[:-1]:
        refs[-1][at:at + ref.shape[0]] = ref[...]
        at += ref.shape[0]


def join(parts):
    total = sum(x.shape[0] for x in parts)
    return small_call(join_kernel, jax.ShapeDtypeStruct((total, *parts[0].shape[1:]), parts[0].dtype), parts, "join")


def masked_kernel(mask, *refs):
    for n, ref in enumerate(refs[:-1]):
        refs[-1][n] = jnp.where(mask[...] > 0, ref[0], jnp.zeros_like(ref[0]))


def masked(mask, parts):
    shape = jax.ShapeDtypeStruct((len(parts), *parts[0].shape[1:]), parts[0].dtype)
    return small_call(masked_kernel, shape, (mask, *parts), "masked")


def finish_kernel(first, *refs):
    pair, factor = refs[-2:]
    join_kernel(*refs[:-1])
    steps = factor.shape[0]
    own = lax.axis_index("pcol") // lax.axis_size("prow")
    factor[own, 0] = first[0]
    for m in range(1, steps):
        factor[lax.rem(own + m, steps), 0] = refs[0][m - 1]


def finish(first, parts):
    total = sum(x.shape[0] for x in parts)
    steps, rows, size = parts[0].shape[0] + 1, *parts[0].shape[1:]
    outs = [jax.ShapeDtypeStruct((total, rows, size), first.dtype),
            jax.ShapeDtypeStruct((steps, 1, rows, size), first.dtype)]
    return small_call(finish_kernel, outs, (first, *parts), "finish")


def hold_kernel(x, _, out):
    del x, out


def hold(x, until):
    return pl.pallas_call(
        hold_kernel,
        out_shape=jax.ShapeDtypeStruct(x.shape, x.dtype),
        in_specs=[HBM, HBM],
        out_specs=HBM,
        input_output_aliases={0: 0},
        cost_estimate=pl.CostEstimate(flops=0, bytes_accessed=1024, transcendentals=0),
        compiler_params=pltpu.CompilerParams(vmem_limit_bytes=SMALL),
        name="hold",
    )(x, until)


def renew_kernel(plan, chips, *refs):
    operands, (trailing, out, rows_full, column, held, out_sems) = refs[:len(plan)], refs[len(plan):]
    steps, size = held.shape[0], held.shape[1]
    rows = size // (2 * chips)
    c, r = lax.axis_index("pcol"), lax.axis_index("prow")
    grid_rows = lax.axis_size("prow")
    own = c // grid_rows
    order = [lax.rem(own + m, steps) for m in range(steps)]
    for ref, places in zip(operands, plan):
        for at, (m, core, k) in enumerate(places):
            source = jnp.bitwise_xor(c, 2 * k + core)
            here = pl.ds(pl.multiple_of(source * rows, rows), rows)
            if m is None:
                column[here] = ref[at]
            else:
                rows_full[m, here] = ref[at]
    for m in range(steps):
        product = lax.dot_general(rows_full[m], column[...], TRANSPOSED, preferred_element_type=jnp.float32)
        before = trailing[order[m], 0, 0, 0]
        renewed = (before.astype(jnp.float32) - product).astype(held.dtype)
        held[m] = jnp.where(order[m] * grid_rows + r >= c, renewed, before)
        pltpu.make_async_copy(held.at[m], out.at[order[m], 0, 0, 0], out_sems.at[m]).start()
    for m in range(steps):
        pltpu.make_async_copy(held.at[m], out.at[order[m], 0, 0, 0], out_sems.at[m]).wait()


def renew(trailing, chips, operands, plan):
    steps, size = trailing.shape[0], trailing.shape[-1]
    tiles = pltpu.VMEM((steps, size, size), trailing.dtype)
    args = (*operands, trailing)
    return pl.pallas_call(
        functools.partial(renew_kernel, plan, chips),
        out_shape=jax.ShapeDtypeStruct(trailing.shape, trailing.dtype),
        in_specs=[VMEM] * len(args),
        out_specs=HBM,
        scratch_shapes=[
            tiles,
            pltpu.VMEM((size, size), trailing.dtype),
            tiles,
            pltpu.SemaphoreType.DMA((steps,)),
        ],
        compiler_params=pltpu.CompilerParams(vmem_limit_bytes=LIMIT),
        name="renew",
    )(*args)


def body(panel, diag_inv, nonzero, trailing):
    grid_rows, grid_cols = lax.axis_size("prow"), lax.axis_size("pcol")
    chips = grid_cols // 2
    classes = max(1, grid_cols // grid_rows)
    steps = panel.shape[0]
    mask, slabs, rests = solve(panel, diag_inv, nonzero, classes)
    slabs = list(slabs)

    def kind(k):
        return 2 * k // grid_rows

    def gather(parts, relay, ks, held):
        for k in ks:
            low = k & -k
            relayed = relay and low != k and kind(low) == 0
            source = held[k ^ low] if relayed else parts[kind(k)]
            held[k] = swap(source, "pcol", 2 * low if relayed else 2 * k)
        return held

    top = chips // 2
    near = gather(slabs, PREL, range(1, chips), {0: slabs[0]})
    half = max(1, chips // GROUPS)
    firsts = [masked(mask, [near[k] for k in range(n, n + half)]) for n in range(0, chips, half)]
    marks = {"p1": near[1], "p2": near[top], "p3": near[chips - 1], "b": firsts[-1], "a": firsts[0]}
    own_rest = rests[0][0]
    if G1:
        own_rest = hold(own_rest, marks[G1])
    close = [k for k in range(1, chips) if kind(k) == 0]
    far = [k for k in range(1, chips) if kind(k) != 0]
    rest = gather([own_rest], QREL, close, {0: own_rest})
    cuts = CUTS(steps)
    pieces = []
    for i in range(len(cuts)):
        parts = [None] + [row[i] for row in rests[1:]]
        if G2 and parts[1:]:
            parts[1] = hold(parts[1], marks[G2])
        pieces.append(gather(parts, QREL, far, {}))
    operands, plan = [], []

    def use(x, places):
        operands.append(x)
        plan.append(tuple(places))

    def both(x, places):
        use(x, [(m, 0, k) for m, k in places])
        use(swap(x, "pcol", 1), [(m, 1, k) for m, k in places])

    for n, first in enumerate(firsts):
        group = range(n * half, (n + 1) * half)
        if XY == "hyper":
            mine = first
            bit = grid_rows // 2
            while bit > 1:
                mine = choose(bit, mine, swap(mine, "prow", bit))
                bit //= 2
            if GX and n == GX[0]:
                mine = hold(mine, pieces[0][top])
            keep, packed = pack(mine, swap(mine, "prow", 1), first)
        else:
            keep, packed = pick([first] + [swap(first, "prow", k) for k in range(1, grid_rows)])
        use(keep, [(None, 0, k) for k in group])
        use(first, [(0, 0, k) for k in group])
        use(swap(packed, "pcol", 1), [(None, 1, k) for k in group] + [(0, 1, k) for k in group])
    joined = [0] + close
    pair, factor = finish(firsts[0], [rest[k] for k in joined])
    both(pair, [(m, k) for k in joined for m in range(1, steps)])
    for k in far:
        m = 1
        for i, cut in enumerate(cuts):
            both(pieces[i][k], [(m + j, k) for j in range(cut)])
            m += cut
    renewed = renew(trailing, chips, operands, plan)
    return factor, renewed


GX = None


PREL = False
QREL = True
GROUPS = 2
G1 = 'b'
G2 = None
XY = 'hyper'


def CUTS(steps):
    return [steps - 1]


def solution(mesh):
    placed = (
        P(None, "prow", "pcol", None),
        P(),
        P(None, "prow"),
        P(None, "prow", None, "pcol", None, None),
    )
    return jax.shard_map(
        body,
        mesh=mesh,
        in_specs=placed,
        out_specs=(P(None, "prow", "pcol", None), P(None, "prow", None, "pcol", None, None)),
        check_vma=False,
    )
```
